128 devices in a mesh: seq: 16 (over x, z), mp: 8 (over y, core).
Axes of the slice: x: 4, y: 4, z: 4, core: 2. Of those that a mesh axis runs over, the one named last changes fastest.
Arguments:
- latents: bfloat16 [1024, 1280], P('seq'), may hold values from -6 to 6
- key_weight: bfloat16 [1280, 8192], P(None, 'mp'), may hold values from -0.15625 to 0.15625
- value_weight: bfloat16 [1280, 8192], P(None, 'mp'), may hold values from -0.15625 to 0.15625
- queries: bfloat16 [32768, 8192], P('seq', 'mp'), may hold values from -6 to 6
- upstream: bfloat16 [32768, 8192], P('seq', 'mp'), may hold values from -6 to 6
- gate: float32 [8192], P('mp'), may hold values from -1.5 to 1.5
- media: int32 [32, 4], P('seq'), may hold values from 0 to 15, all different within a row
- frame_slot: int32 [16], replicated, may hold values from 0 to 15, each once
- lengths: int32 [32], P('seq'), may hold values from 1 to 1024, 16384 in all
Outputs:
- query_grad: bfloat16 [32768, 8192], P('seq', 'mp')
- key_grad: float32 [1280, 8192], P('seq', 'mp')
- value_grad: float32 [1280, 8192], P('seq', 'mp')
The draws below stay inside these ranges and needn't reach their ends.
Inputs may be any that keep to these rules, and one draw needn't show every extreme that they name: `media`: each group names 4 different frames; every frame is named by some group. `frame_slot`: each slot holds exactly one frame. `lengths`: some group is full.
All inputs are finite; a program needn't handle non-finite values.
Results may differ from the reference program's by a relative error of at most 0.009.
Values may be sent and summed in bfloat16 or wider, within the bound.
No kernel may reach another device: no remote copies, remote signals or barrier semaphores. Data moves between devices by JAX's collectives and lax.ppermute only.
A program may use at most 128 MiB of HBM per device.

```python
import math
import jax
import jax.numpy as jnp
import numpy as np
from jax import lax

HEADS = 64
HEAD_DIM = 128
LATENTS = 64
VISION_D = 1280
MEDIA = 4
GROUP_LEN = 1024
D = 8192
FRAMES = 16
GROUPS = 32
TOKENS = 32768


def levels(rng, shape, split, smallest, top_value):
    factor_of, own = 1.0, jax.random.fold_in(rng, 6)
    for axis_at, parts in split:
        steps = jnp.exp(jax.random.uniform(jax.random.fold_in(own, axis_at), (parts,), jnp.float32, smallest / len(split), top_value / len(split)))
        factor_of = factor_of * jnp.repeat(steps, shape[axis_at] // parts).reshape([-1 if axis == axis_at else 1 for axis in range(len(shape))])
    return factor_of


def picks_of(rng, rows, count, top, lift):
    ranking = jax.random.permutation(jax.random.fold_in(rng, 1), count)
    boost = ranking
    for power in range(3):
        boost = boost * boost // count
    boost = boost * lift // count
    tickets = jax.random.randint(jax.random.fold_in(rng, 2), (rows, count), 0, 4096) + boost
    fixed_rows = jax.random.permutation(jax.random.fold_in(rng, 3), rows)[jnp.arange(count) % rows]
    tickets = jnp.where(jnp.arange(rows)[:, None] == fixed_rows[None, :], 1 << 14, tickets)
    score = tickets * count + jnp.arange(count)
    return lax.top_k(score.astype(jnp.int32), top)[1].astype(jnp.int32)


def length_profile(number_of, total, limit, lean):
    weights = [(1 << 20) // math.isqrt(rank ** lean) + 1 for rank in range(2, number_of + 1)]
    surplus, given = total - limit - (number_of - 1), [1] * (number_of - 1)
    while surplus > 0:
        free = [i for i in range(number_of - 1) if given[i] < limit]
        pool, remaining = sum([weights[i] for i in free]), surplus
        for i in free:
            extra = min(limit - given[i], max(1, remaining * weights[i] // pool), surplus)
            given[i] = given[i] + extra
            surplus = surplus - extra
    return np.array([limit] + given)


def ragged_sizes(own_key, count, total, most, slope):
    if count == 2:
        one = jax.random.randint(own_key, (), max(1, total - most), min(most, total - 1) + 1)
        return jnp.stack([one, total - one])
    sizes = jnp.asarray(length_profile(count, total, most, slope), jnp.int32)
    pairs = (count - 1) // 2
    giver, taker = sizes[1:1 + 2 * pairs:2], sizes[2:2 + 2 * pairs:2]
    room = jnp.minimum(giver - 1, most - taker)
    shifted = jax.random.randint(jax.random.fold_in(own_key, 1), (pairs,), 0, 1 << 20) % (room + 1)
    sizes = sizes.at[1:1 + 2 * pairs:2].set(giver - shifted).at[2:2 + 2 * pairs:2].set(taker + shifted)
    return sizes[jax.random.permutation(jax.random.fold_in(own_key, 2), count)]


def scatter_about(key, extent, spread, reach, split=(), kind=jnp.bfloat16):
    loudness = levels(key, extent, split, -0.22, 0.18) if split else 1.0
    drawn = jax.random.normal(key, extent, jnp.float32) * spread * loudness
    return jnp.minimum(jnp.maximum(drawn, -reach), reach).astype(kind)


def setup_inputs(seed: int = 0) -> dict:
    key_list = jax.random.split(jax.random.key(seed), 10)
    return {
        "latents": scatter_about(key_list[0], (FRAMES * LATENTS, VISION_D), 1.0, 6.0, ((0, 16),)),
        "key_weight": scatter_about(key_list[1], (VISION_D, D), VISION_D ** -0.5, 0.15625, ((1, 8),)),
        "value_weight": scatter_about(key_list[2], (VISION_D, D), VISION_D ** -0.5, 0.15625, ((1, 8),)),
        "queries": scatter_about(key_list[3], (TOKENS, D), 1.0, 6.0, ((0, 16), (1, 8))),
        "upstream": scatter_about(key_list[4], (TOKENS, D), 1.0, 6.0, ((0, 16), (1, 8))),
        "gate": jnp.clip(jax.random.uniform(key_list[5], (D,), jnp.float32, -1.5, 1.5) * levels(key_list[5], (D,), ((0, 8),), -0.4, 0.0), -1.5, 1.5),
        "media": picks_of(key_list[6], GROUPS, FRAMES, MEDIA, 2048),
        "frame_slot": jax.random.permutation(key_list[7], FRAMES).astype(jnp.int32),
        "lengths": ragged_sizes(key_list[8], GROUPS, GROUPS * GROUP_LEN // 2, GROUP_LEN, 2).astype(jnp.int32),
    }


def reference(latents, key_weight, value_weight, queries, upstream, gate, media, frame_slot, lengths):
    both = jnp.concatenate([key_weight, value_weight], axis=1)
    projected = jnp.dot(latents, both, preferred_element_type=jnp.float32)
    kv_table = projected.astype(jnp.bfloat16).reshape(FRAMES, LATENTS, 2 * D)
    gate_tanh = jnp.tanh(gate)
    scale = HEAD_DIM ** -0.5
    positions = jnp.arange(GROUP_LEN)
    query_blocks = queries.reshape(GROUPS, GROUP_LEN, HEADS, HEAD_DIM)
    upstream_blocks = upstream.reshape(GROUPS, GROUP_LEN, D)

    def one_group(carry, group):
        slots = frame_slot[media[group]]
        picked = jnp.take(kv_table, slots, axis=0).reshape(MEDIA * LATENTS, 2 * D)
        keys = picked[:, :D].reshape(-1, HEADS, HEAD_DIM).astype(jnp.float32)
        values = picked[:, D:].reshape(-1, HEADS, HEAD_DIM).astype(jnp.float32)
        query_now = query_blocks[group].astype(jnp.float32)
        live = positions < lengths[group]
        dout = jnp.where(live[:, None], gate_tanh * upstream_blocks[group].astype(jnp.float32), 0.0).astype(jnp.bfloat16)
        dout_full = lax.optimization_barrier(dout).reshape(GROUP_LEN, HEADS, HEAD_DIM).astype(jnp.float32)
        scores = jnp.einsum('thd,khd->htk', query_now, keys) * scale
        probs = jax.nn.softmax(scores, axis=-1)
        probs_b = lax.optimization_barrier(probs.astype(jnp.bfloat16)).astype(jnp.float32)
        output = jnp.einsum('htk,khd->thd', probs_b, values)
        delta = jnp.sum(dout_full * output, axis=-1)
        dprob = jnp.einsum('thd,khd->htk', dout_full, values)
        dscore = lax.optimization_barrier((probs * (dprob - delta.T[:, :, None])).astype(jnp.bfloat16)).astype(jnp.float32)
        query_part = (jnp.einsum('htk,khd->thd', dscore, keys) * scale).astype(jnp.bfloat16).reshape(GROUP_LEN, D)
        key_part = jnp.einsum('htk,thd->khd', dscore, query_now) * scale
        value_part = jnp.einsum('htk,thd->khd', probs_b, dout_full)
        contrib = jnp.concatenate([key_part.reshape(-1, D), value_part.reshape(-1, D)], axis=1).reshape(MEDIA, LATENTS, 2 * D)
        return carry.at[slots].add(contrib), query_part

    start = jnp.zeros((FRAMES, LATENTS, 2 * D), jnp.float32)
    grads, query_parts = lax.scan(one_group, start, jnp.arange(GROUPS))
    grads_b = grads.reshape(FRAMES * LATENTS, 2 * D).astype(jnp.bfloat16)
    dims = (((0,), (0,)), ((), ()))
    key_grad = lax.dot_general(latents, grads_b[:, :D], dims, preferred_element_type=jnp.float32)
    value_grad = lax.dot_general(latents, grads_b[:, D:], dims, preferred_element_type=jnp.float32)
    return query_parts.reshape(TOKENS, D), key_grad, value_grad
```

```python
import functools
import math

import jax
import jax.numpy as jnp
from jax import lax
from jax.experimental import pallas as pl
from jax.experimental.pallas import tpu as pltpu
from jax.sharding import PartitionSpec as P

HEAD_DIM = 128
LATENTS = 64
SIDE = 4
PAIR = 2 * HEAD_DIM
TOKEN_BLOCK = 256
ONES = (((1,), (1,)), ((), ()))
ZEROS = (((0,), (0,)), ((), ()))


def shift(array, major, minor, mp):
    pairs = []
    for x in range(SIDE):
        for z in range(SIDE):
            for m in range(mp):
                dx, dz = (major, minor) if m % 2 == 0 else (minor, major)
                to = ((x + dx) % SIDE) * SIDE + (z + dz) % SIDE
                pairs.append(((x * SIDE + z) * mp + m, to * mp + m))
    return lax.ppermute(array, ("seq", "mp"), pairs)


def swap_cores(array, mp):
    return lax.ppermute(array, "mp", [(m, m ^ 1) for m in range(mp)])


def gather_latents(latents, mp):
    half = latents.shape[1] // 2
    mine = jnp.where(lax.axis_index("mp") % 2 == 0, latents[:, :half], latents[:, half:])
    far = shift(mine, 2, 0, mp)
    near = [shift(mine, step, 0, mp) for step in (1, 3)]
    line = jnp.concatenate([mine, near[0], far, near[1]], axis=0)
    far = shift(line, 0, 2, mp)
    near = [shift(line, 0, step, mp) for step in (1, 3)]
    fetched = [line, near[0], far, near[1]]
    return fetched + [swap_cores(part, mp) for part in fetched]


def attention_kernel(
    media, frame_slot, lengths, place, *refs
):
    parts = refs[:8]
    gate, key_weight, value_weight, queries, upstream, query_grad = refs[8:14]
    messages = refs[14:22]
    picked, picked_t, keys, values, key_sum, value_sum, key_part, value_part, rows_key, rows_value = refs[22:]
    groups, named = media.shape
    group_keys = named * LATENTS
    group_len = queries.shape[0] // groups
    half = parts[0].shape[1]
    seq, core = place[0], place[1]
    x, z = seq // SIDE, seq % SIDE
    scale = HEAD_DIM ** -0.5
    sharpness = scale * math.log2(math.e)

    @pl.when(pl.program_id(0) == 0)
    def _():
        for group in range(groups):
            for name in range(named):
                slot = frame_slot[media[group, name]]
                dx = (x - slot // SIDE + SIDE) % SIDE
                dz = (z - slot % SIDE + SIDE) % SIDE
                to = pl.ds((group * named + name) * LATENTS, LATENTS)
                for side in range(2):
                    minor, major = (dx, dz) if side == 0 else (dz, dx)
                    start = pl.ds(pl.multiple_of(minor * LATENTS, LATENTS), LATENTS)
                    first = jnp.where(core == side, 0, 4)
                    for at in range(8):

                        @pl.when(first + major == at)
                        def _():
                            picked[to, side * half : (side + 1) * half] = parts[at][start, :]

        picked_t[...] = picked[...].T

    keys[...] = jnp.dot(picked[...], key_weight[...], preferred_element_type=jnp.float32).astype(jnp.bfloat16)
    values[...] = jnp.dot(picked[...], value_weight[...], preferred_element_type=jnp.float32).astype(jnp.bfloat16)
    gate_tanh = jnp.tanh(gate[...])

    for group in range(groups):
        rows = slice(group * group_keys, (group + 1) * group_keys)
        length = lengths[group]
        blocks = (length + TOKEN_BLOCK - 1) // TOKEN_BLOCK
        key_sum[...] = jnp.zeros_like(key_sum)
        value_sum[...] = jnp.zeros_like(value_sum)

        def block(step, carry):
            at = pl.multiple_of(step * TOKEN_BLOCK, TOKEN_BLOCK)
            tokens = pl.ds(group * group_len + at, TOKEN_BLOCK)
            live = lax.broadcasted_iota(jnp.int32, (TOKEN_BLOCK, HEAD_DIM), 0) + at < length
            for head in range(2):
                cols = slice(head * HEAD_DIM, (head + 1) * HEAD_DIM)
                k, v = keys[rows, cols], values[rows, cols]
                q = queries[tokens, cols]
                gated = gate_tanh[:, cols] * upstream[tokens, cols].astype(jnp.float32)
                dout = jnp.where(live, gated, 0.0).astype(jnp.bfloat16)
                scores = lax.dot_general(k, q, ONES, preferred_element_type=jnp.float32)
                dprob = lax.dot_general(v, dout, ONES, preferred_element_type=jnp.float32)
                top = jnp.max(scores, axis=0, keepdims=True)
                powers = jnp.exp2((scores - top) * sharpness)
                probs = powers * (1.0 / jnp.sum(powers, axis=0, keepdims=True))
                delta = jnp.sum(probs * dprob, axis=0, keepdims=True)
                dscore = (probs * (dprob - delta)).astype(jnp.bfloat16)
                probs_b = probs.astype(jnp.bfloat16)
                key_sum[:, cols] += jnp.dot(dscore, q, preferred_element_type=jnp.float32)
                value_sum[:, cols] += jnp.dot(probs_b, dout, preferred_element_type=jnp.float32)
                grad = lax.dot_general(dscore, k, ZEROS, preferred_element_type=jnp.float32)
                query_grad[tokens, cols] = (grad * scale).astype(jnp.bfloat16)
            return carry

        lax.fori_loop(0, blocks, block, 0)

        def blank(step, carry):
            tokens = pl.ds(group * group_len + pl.multiple_of(step * TOKEN_BLOCK, TOKEN_BLOCK), TOKEN_BLOCK)
            query_grad[tokens, :] = jnp.zeros((TOKEN_BLOCK, PAIR), jnp.bfloat16)
            return carry

        lax.fori_loop(blocks, group_len // TOKEN_BLOCK, blank, 0)
        key_part[rows, :] = (key_sum[...] * scale).astype(jnp.bfloat16)
        value_part[rows, :] = value_sum[...].astype(jnp.bfloat16)

    rows_key[...] = jnp.dot(picked_t[...], key_part[...], preferred_element_type=jnp.float32).astype(jnp.bfloat16)
    rows_value[...] = jnp.dot(picked_t[...], value_part[...], preferred_element_type=jnp.float32).astype(jnp.bfloat16)
    share = rows_key.shape[0] // (SIDE * SIDE)
    for major in range(SIDE):
        for minor in range(SIDE):
            dx = jnp.where(core == 0, major, minor)
            dz = jnp.where(core == 0, minor, major)
            owner = ((x + dx) % SIDE) * SIDE + (z + dz) % SIDE
            source = pl.ds(pl.multiple_of(owner * share, 16), share)
            to = slice(minor * share, (minor + 1) * share)
            messages[major][to, :] = rows_key[source, :]
            messages[SIDE + major][to, :] = rows_value[source, :]


def attention(parts, key_weight, value_weight, queries, upstream, gate, media, frame_slot, lengths, place):
    tokens, width = queries.shape
    vision = key_weight.shape[0]
    steps = width // PAIR
    picked_rows = media.shape[0] * media.shape[1] * LATENTS
    group_keys = media.shape[1] * LATENTS
    whole = lambda array: pl.BlockSpec(array.shape, lambda step, *_: (0, 0))
    columns = lambda rows: pl.BlockSpec((rows, PAIR), lambda step, *_: (0, step))
    quarter = vision // SIDE
    bf16, f32 = jnp.bfloat16, jnp.float32
    return pl.pallas_call(
        attention_kernel,
        grid_spec=pltpu.PrefetchScalarGridSpec(
            num_scalar_prefetch=4,
            grid=(steps,),
            in_specs=[whole(part) for part in parts]
            + [columns(1), columns(vision), columns(vision), columns(tokens), columns(tokens)],
            out_specs=[columns(tokens)] + [columns(quarter)] * (2 * SIDE),
            scratch_shapes=[
                pltpu.VMEM((picked_rows, vision), bf16),
                pltpu.VMEM((vision, picked_rows), bf16),
                pltpu.VMEM((picked_rows, PAIR), bf16),
                pltpu.VMEM((picked_rows, PAIR), bf16),
                pltpu.VMEM((group_keys, PAIR), f32),
                pltpu.VMEM((group_keys, PAIR), f32),
                pltpu.VMEM((picked_rows, PAIR), bf16),
                pltpu.VMEM((picked_rows, PAIR), bf16),
                pltpu.VMEM((vision, PAIR), bf16),
                pltpu.VMEM((vision, PAIR), bf16),
            ],
        ),
        out_shape=[jax.ShapeDtypeStruct((tokens, width), bf16)]
        + [jax.ShapeDtypeStruct((quarter, width), bf16)] * (2 * SIDE),
        compiler_params=pltpu.CompilerParams(vmem_limit_bytes=48 * 1024 * 1024),
    )(media, frame_slot, lengths, place, *parts, gate[None, :], key_weight, value_weight, queries, upstream)


def add(*arrays):
    return functools.reduce(jnp.add, [array.astype(jnp.float32) for array in arrays])


def scatter_sum(messages, mp):
    key, value = messages[:SIDE], messages[SIDE:]
    share = key[0].shape[0] // SIDE
    bf16 = jnp.bfloat16
    key_far = shift(key[2], 1, 0, mp)
    value_far = shift(value[2], 3, 0, mp)
    value_near = shift(value[1], 1, 0, mp)
    key_near = shift(key[3], 3, 0, mp)
    key_on = shift(add(key[1], key_far).astype(bf16), 1, 0, mp)
    value_on = shift(add(value[3], value_far).astype(bf16), 3, 0, mp)
    key_rows = add(key[0], key_near, key_on)
    value_rows = add(value[0], value_near, value_on)
    both = [
        jnp.concatenate([key_rows[at * share : (at + 1) * share], value_rows[at * share : (at + 1) * share]], axis=0)
        for at in range(SIDE)
    ]
    came = [shift(both[at].astype(bf16), 0, at, mp) for at in (2, 1, 3)]
    total = add(both[0], *came)
    return total[:share], total[share:]


def local(latents, key_weight, value_weight, queries, upstream, gate, media, frame_slot, lengths, *, mp):
    parts = gather_latents(latents, mp)
    place = jnp.stack([lax.axis_index("seq"), lax.axis_index("mp") % 2]).astype(jnp.int32)
    query_grad, *messages = attention(
        parts, key_weight, value_weight, queries, upstream, gate, media, frame_slot, lengths, place
    )
    key_grad, value_grad = scatter_sum(messages, mp)
    return query_grad, key_grad, value_grad


def solution(mesh):
    in_specs = (
        P("seq", None),
        P(None, "mp"),
        P(None, "mp"),
        P("seq", "mp"),
        P("seq", "mp"),
        P("mp"),
        P("seq", None),
        P(),
        P("seq"),
    )
    out_specs = (P("seq", "mp"), P("seq", "mp"), P("seq", "mp"))
    body = functools.partial(local, mp=mesh.shape["mp"])
    return jax.shard_map(body, mesh=mesh, in_specs=in_specs, out_specs=out_specs, check_vma=False)
```

```python
import functools
import math

import jax
import jax.numpy as jnp
from jax import lax
from jax.experimental import pallas as pl
from jax.experimental.pallas import tpu as pltpu
from jax.sharding import PartitionSpec as P

HEAD_DIM = 128
LATENTS = 64
SIDE = 4
HEADS = 2
PAIR = HEADS * HEAD_DIM
TOKEN_BLOCK = 512
ONES = (((1,), (1,)), ((), ()))
ZEROS = (((0,), (0,)), ((), ()))
BF16 = jnp.bfloat16
F32 = jnp.float32


def shift(array, major, minor, mp):
    pairs = []
    for x in range(SIDE):
        for z in range(SIDE):
            for m in range(mp):
                dx, dz = (major, minor) if m % 2 == 0 else (minor, major)
                to = ((x + dx) % SIDE) * SIDE + (z + dz) % SIDE
                pairs.append(((x * SIDE + z) * mp + m, to * mp + m))
    return lax.ppermute(array, ("seq", "mp"), pairs)


def swap_cores(array, mp):
    return lax.ppermute(array, "mp", [(m, m ^ 1) for m in range(mp)])


def gather_latents(latents, aside, mp):
    half = latents.shape[1] // 2
    mine = jnp.where(lax.axis_index("mp") % 2 == 0, latents[:, :half], latents[:, half:])
    far = shift(mine, 2, 0, mp)
    near = [shift(mine, step, 0, mp) for step in (1, 3)]
    line = jnp.concatenate([mine, near[0], far, near[1]], axis=0)
    far = shift(line, 0, 2, mp)
    near = [shift(line, 0, step, mp) for step in (1, 3)]
    line, aside = lax.optimization_barrier((line, aside))
    fetched = [line, near[0], far, near[1]]
    return fetched + [swap_cores(part, mp) for part in fetched], aside


def numbers_at(groups, named, frames):
    slots = groups * named
    lengths = slots + frames
    return slots, lengths, lengths + groups


def pick(numbers, parts, picked, turned, picked_t, groups, named):
    slots_at, lengths_at, place_at = numbers_at(groups, named, SIDE * SIDE)
    half = parts[0].shape[1]
    seq, core = numbers[place_at], numbers[place_at + 1]
    x, z = seq // SIDE, seq % SIDE
    for name in range(groups * named):
        slot = numbers[slots_at + numbers[name]]
        dx = (x - slot // SIDE + SIDE) % SIDE
        dz = (z - slot % SIDE + SIDE) % SIDE
        to = pl.ds(name * LATENTS, LATENTS)
        for side in range(2):
            minor, major = (dx, dz) if side == 0 else (dz, dx)
            start = pl.ds(pl.multiple_of(minor * LATENTS, LATENTS), LATENTS)
            first = jnp.where(core == side, 0, 4)
            for at in range(8):

                @pl.when(first + major == at)
                def _():
                    picked[to, side * half : (side + 1) * half] = parts[at][start, :]

    turned[...] = picked[...].T
    share = turned.shape[0] // (SIDE * SIDE)
    for major in range(SIDE):
        for minor in range(SIDE):
            dx = jnp.where(core == 0, major, minor)
            dz = jnp.where(core == 0, minor, major)
            owner = ((x + dx) % SIDE) * SIDE + (z + dz) % SIDE
            to = (major * SIDE + minor) * share
            picked_t[to : to + share, :] = turned[pl.ds(pl.multiple_of(owner * share, 16), share), :]


def backward(numbers, picked, picked_t, gate_tanh, key_weight, value_weight, queries, upstream, query_grad, scratch, groups, named):
    keys, values, key_sum, value_sum, key_part, value_part = scratch
    lengths_at = numbers_at(groups, named, SIDE * SIDE)[1]
    group_keys = named * LATENTS
    group_len = queries.shape[0] // groups
    scale = HEAD_DIM**-0.5
    sharpness = scale * math.log2(math.e)
    keys[...] = jnp.dot(picked[...], key_weight[...], preferred_element_type=F32).astype(BF16)
    values[...] = jnp.dot(picked[...], value_weight[...], preferred_element_type=F32).astype(BF16)
    heads = [slice(head * HEAD_DIM, (head + 1) * HEAD_DIM) for head in range(HEADS)]

    for group in range(groups):
        rows = slice(group * group_keys, (group + 1) * group_keys)
        length = numbers[lengths_at + group]
        blocks = (length + TOKEN_BLOCK - 1) // TOKEN_BLOCK
        key_sum[...] = jnp.zeros_like(key_sum)
        value_sum[...] = jnp.zeros_like(value_sum)

        def block(step, carry):
            at = pl.multiple_of(step * TOKEN_BLOCK, TOKEN_BLOCK)
            tokens = pl.ds(group * group_len + at, TOKEN_BLOCK)
            live = lax.broadcasted_iota(jnp.int32, (TOKEN_BLOCK, HEAD_DIM), 0) + at < length
            made = []
            for cols in heads:
                q = queries[tokens, cols]
                gated = gate_tanh[:, cols] * upstream[tokens, cols].astype(F32)
                dout = jnp.where(live, gated, 0.0).astype(BF16)
                scores = lax.dot_general(keys[rows, cols], q, ONES, preferred_element_type=F32)
                dprob = lax.dot_general(values[rows, cols], dout, ONES, preferred_element_type=F32)
                made.append((cols, q, dout, scores, dprob))
            for cols, q, dout, scores, dprob in made:
                top = jnp.max(scores, axis=0, keepdims=True)
                powers = jnp.exp2((scores - top) * sharpness)
                probs = powers * (1.0 / jnp.sum(powers, axis=0, keepdims=True))
                delta = jnp.sum(probs * dprob, axis=0, keepdims=True)
                dscore = (probs * (dprob - delta)).astype(BF16)
                key_sum[:, cols] += jnp.dot(dscore, q, preferred_element_type=F32)
                value_sum[:, cols] += jnp.dot(probs.astype(BF16), dout, preferred_element_type=F32)
                grad = lax.dot_general(dscore, keys[rows, cols], ZEROS, preferred_element_type=F32)
                query_grad[tokens, cols] = (grad * scale).astype(BF16)
            return carry

        lax.fori_loop(0, blocks, block, 0)

        def blank(step, carry):
            tokens = pl.ds(group * group_len + pl.multiple_of(step * TOKEN_BLOCK, TOKEN_BLOCK), TOKEN_BLOCK)
            query_grad[tokens, :] = jnp.zeros((TOKEN_BLOCK, PAIR), BF16)
            return carry

        lax.fori_loop(blocks, group_len // TOKEN_BLOCK, blank, 0)
        key_part[rows, :] = (key_sum[...] * scale).astype(BF16)
        value_part[rows, :] = value_sum[...].astype(BF16)

    quarter = picked_t.shape[0] // SIDE
    for major in range(SIDE):
        rows = slice(major * quarter, (major + 1) * quarter)
        for part in (key_part, value_part):
            product = jnp.dot(picked_t[rows, :], part[...], preferred_element_type=F32)
            yield major, part is value_part, product.astype(BF16)


def first_kernel(groups, named, numbers, *refs):
    parts, (gate_tanh, key_weight, value_weight, queries, upstream) = refs[:8], refs[8:13]
    query_grad, messages, (picked, picked_t), turned, scratch = refs[13], refs[14:18], refs[18:20], refs[20], refs[21:]

    @pl.when(pl.program_id(0) == 0)
    def _():
        pick(numbers, parts, picked, turned, picked_t, groups, named)

    share = picked.shape[1] // (SIDE * SIDE)
    for major, second, product in backward(
        numbers, picked, picked_t, gate_tanh, key_weight, value_weight, queries, upstream, query_grad, scratch, groups, named
    ):
        for minor in range(SIDE):
            to = (2 * minor + second) * share
            messages[major][to : to + share, :] = product[minor * share : (minor + 1) * share]


def second_kernel(groups, named, numbers, *refs):
    picked, picked_t, gate_tanh, key_weight, value_weight, queries, upstream = refs[:7]
    query_grad, messages, scratch = refs[8], refs[9:17], refs[17:]
    for major, second, product in backward(
        numbers, picked, picked_t, gate_tanh, key_weight, value_weight, queries, upstream, query_grad, scratch, groups, named
    ):
        messages[second * SIDE + major][...] = product


def attention(numbers, latents, gate_tanh, key_weight, value_weight, queries, upstream, query_grad, groups, named):
    first = query_grad is None
    tokens, width = queries.shape
    vision = key_weight.shape[0]
    steps = width // PAIR // 2
    offset = 0 if first else steps
    picked_rows = groups * named * LATENTS
    group_keys = named * LATENTS
    quarter = vision // SIDE
    whole = lambda shape: pl.BlockSpec(shape, lambda step, *_: (0, 0))
    columns = lambda rows: pl.BlockSpec((rows, PAIR), lambda step, *_: (0, step + offset))
    message = lambda rows: pl.BlockSpec((rows, PAIR), lambda step, *_: (0, step))
    shape = jax.ShapeDtypeStruct
    in_specs = [whole(part.shape) for part in latents]
    in_specs += [columns(1), columns(vision), columns(vision), columns(tokens), columns(tokens)]
    inputs = [numbers, *latents, gate_tanh, key_weight, value_weight, queries, upstream]
    out_specs, out_shape = [columns(tokens)], [shape((tokens, width), BF16)]
    scratch = [
        pltpu.VMEM((picked_rows, PAIR), BF16),
        pltpu.VMEM((picked_rows, PAIR), BF16),
        pltpu.VMEM((group_keys, PAIR), F32),
        pltpu.VMEM((group_keys, PAIR), F32),
        pltpu.VMEM((picked_rows, PAIR), BF16),
        pltpu.VMEM((picked_rows, PAIR), BF16),
    ]
    if first:
        out_specs += [message(2 * quarter)] * SIDE + [whole((picked_rows, vision)), whole((vision, picked_rows))]
        out_shape += [shape((2 * quarter, width // 2), BF16)] * SIDE
        out_shape += [shape((picked_rows, vision), BF16), shape((vision, picked_rows), BF16)]
        scratch = [pltpu.VMEM((vision, picked_rows), BF16)] + scratch
        aliases = {}
    else:
        in_specs.append(pl.BlockSpec(memory_space=pl.ANY))
        inputs.append(query_grad)
        out_specs += [message(quarter)] * (2 * SIDE)
        out_shape += [shape((quarter, width // 2), BF16)] * (2 * SIDE)
        aliases = {len(inputs) - 1: 0}
    return pl.pallas_call(
        functools.partial(first_kernel if first else second_kernel, groups, named),
        grid_spec=pltpu.PrefetchScalarGridSpec(
            num_scalar_prefetch=1, grid=(steps,), in_specs=in_specs, out_specs=out_specs, scratch_shapes=scratch
        ),
        out_shape=out_shape,
        input_output_aliases=aliases,
        compiler_params=pltpu.CompilerParams(vmem_limit_bytes=40 * 1024 * 1024),
        cost_estimate=pl.CostEstimate(flops=10**10, bytes_accessed=10**7, transcendentals=0),
    )(*inputs)


def add(*arrays):
    return functools.reduce(jnp.add, [array.astype(F32) for array in arrays])


def last_sum(shares, mp):
    came = [shift(shares[at].astype(BF16), 0, at, mp) for at in (2, 1, 3)]
    total = add(shares[0], *came)
    rows = total.shape[0] // 2
    return total[:rows], total[rows:]


def local(latents, key_weight, value_weight, queries, upstream, gate, media, frame_slot, lengths, *, mp):
    groups, named = media.shape
    place = jnp.stack([lax.axis_index("seq"), lax.axis_index("mp") % 2]).astype(jnp.int32)
    aside = (jnp.concatenate([media.reshape(-1), frame_slot, lengths, place]), jnp.tanh(gate)[None, :])
    parts, (numbers, gate_tanh) = gather_latents(latents, aside, mp)
    rest = (gate_tanh, key_weight, value_weight, queries, upstream)
    query_grad, *joined, picked, picked_t = attention(numbers, parts, *rest, None, groups, named)
    came = [shift(joined[at], at, 0, mp) for at in (2, 1, 3)]

    query_grad, *messages = attention(numbers, (picked, picked_t), *rest, query_grad, groups, named)
    rows, messages = lax.optimization_barrier((add(joined[0], *came), messages))
    key, value = messages[:SIDE], messages[SIDE:]
    key_far = shift(key[2], 1, 0, mp)
    value_far = shift(value[2], 3, 0, mp)
    value_near = shift(value[1], 1, 0, mp)
    key_near = shift(key[3], 3, 0, mp)

    share = rows.shape[0] // SIDE
    first = last_sum([rows[at * share : (at + 1) * share] for at in range(SIDE)], mp)

    key_on = shift(add(key[1], key_far).astype(BF16), 1, 0, mp)
    value_on = shift(add(value[3], value_far).astype(BF16), 3, 0, mp)
    key_rows = add(key[0], key_near, key_on)
    value_rows = add(value[0], value_near, value_on)
    share //= 2
    cut = lambda array, at: array[at * share : (at + 1) * share]
    second = last_sum([jnp.concatenate([cut(key_rows, at), cut(value_rows, at)], axis=0) for at in range(SIDE)], mp)
    key_grad, value_grad = [jnp.concatenate(halves, axis=1) for halves in zip(first, second)]
    return query_grad, key_grad, value_grad


def solution(mesh):
    in_specs = (
        P("seq", None),
        P(None, "mp"),
        P(None, "mp"),
        P("seq", "mp"),
        P("seq", "mp"),
        P("mp"),
        P("seq", None),
        P(),
        P("seq"),
    )
    out_specs = (P("seq", "mp"), P("seq", "mp"), P("seq", "mp"))
    body = functools.partial(local, mp=mesh.shape["mp"])
    return jax.shard_map(body, mesh=mesh, in_specs=in_specs, out_specs=out_specs, check_vma=False)
```

```python
import functools
import math

import jax
import jax.numpy as jnp
from jax import lax
from jax.experimental import pallas as pl
from jax.experimental.pallas import tpu as pltpu
from jax.sharding import PartitionSpec as P

HEAD_DIM = 128
LATENTS = 64
SIDE = 4
HEADS = 2
PAIR = HEADS * HEAD_DIM
TOKEN_BLOCK = 512
ONES = (((1,), (1,)), ((), ()))
ZEROS = (((0,), (0,)), ((), ()))
BF16 = jnp.bfloat16
F32 = jnp.float32


def shift(array, major, minor, mp):
    pairs = []
    for x in range(SIDE):
        for z in range(SIDE):
            for m in range(mp):
                dx, dz = (major, minor) if m % 2 == 0 else (minor, major)
                to = ((x + dx) % SIDE) * SIDE + (z + dz) % SIDE
                pairs.append(((x * SIDE + z) * mp + m, to * mp + m))
    return lax.ppermute(array, ("seq", "mp"), pairs)


def swap_cores(array, mp):
    return lax.ppermute(array, "mp", [(m, m ^ 1) for m in range(mp)])


def gather_latents(latents, numbers, gate_tanh, arrays, groups, named, mp):
    half = latents.shape[1] // 2
    mine = jnp.where(lax.axis_index("mp") % 2 == 0, latents[:, :half], latents[:, half:])
    far = shift(mine, 2, 0, mp)
    near = [shift(mine, step, 0, mp) for step in (1, 3)]
    line = jnp.concatenate([mine, near[0], far, near[1]], axis=0)
    line, numbers, gate_tanh = lax.optimization_barrier((line, numbers, gate_tanh))
    far = shift(line, 0, 2, mp)
    near = [shift(line, 0, step, mp) for step in (1, 3)]
    *arrays, numbers = stage(numbers, gate_tanh, *arrays, groups, named)
    *fetched, numbers = lax.optimization_barrier((line, near[0], far, near[1], numbers))
    return fetched + [swap_cores(part, mp) for part in fetched], numbers, arrays


def numbers_at(groups, named, frames):
    slots = groups * named
    lengths = slots + frames
    return slots, lengths, lengths + groups


def pick(numbers, parts, picked, turned, picked_t, groups, named):
    slots_at, lengths_at, place_at = numbers_at(groups, named, SIDE * SIDE)
    half = parts[0].shape[1]
    seq, core = numbers[place_at], numbers[place_at + 1]
    x, z = seq // SIDE, seq % SIDE
    for name in range(groups * named):
        slot = numbers[slots_at + numbers[name]]
        dx = (x - slot // SIDE + SIDE) % SIDE
        dz = (z - slot % SIDE + SIDE) % SIDE
        to = pl.ds(name * LATENTS, LATENTS)
        for side in range(2):
            minor, major = (dx, dz) if side == 0 else (dz, dx)
            start = pl.ds(pl.multiple_of(minor * LATENTS, LATENTS), LATENTS)
            first = jnp.where(core == side, 0, 4)
            for at in range(8):

                @pl.when(first + major == at)
                def _():
                    picked[to, side * half : (side + 1) * half] = parts[at][start, :]

    turned[...] = picked[...].T
    share = turned.shape[0] // (SIDE * SIDE)
    for major in range(SIDE):
        for minor in range(SIDE):
            dx = jnp.where(core == 0, major, minor)
            dz = jnp.where(core == 0, minor, major)
            owner = ((x + dx) % SIDE) * SIDE + (z + dz) % SIDE
            to = (major * SIDE + minor) * share
            picked_t[to : to + share, :] = turned[pl.ds(pl.multiple_of(owner * share, 16), share), :]


def backward(numbers, picked, picked_t, key_weight, value_weight, queries, upstream, query_grad, scratch, groups, named):
    keys, values, key_sum, value_sum, key_part, value_part = scratch
    lengths_at = numbers_at(groups, named, SIDE * SIDE)[1]
    group_keys = named * LATENTS
    group_len = queries.shape[0] // groups
    scale = HEAD_DIM**-0.5
    sharpness = scale * math.log2(math.e)
    keys[...] = jnp.dot(picked[...], key_weight[...], preferred_element_type=F32).astype(BF16)
    values[...] = jnp.dot(picked[...], value_weight[...], preferred_element_type=F32).astype(BF16)
    heads = [slice(head * HEAD_DIM, (head + 1) * HEAD_DIM) for head in range(HEADS)]

    for group in range(groups):
        rows = slice(group * group_keys, (group + 1) * group_keys)
        length = numbers[lengths_at + group]
        blocks = (length + TOKEN_BLOCK - 1) // TOKEN_BLOCK
        key_sum[...] = jnp.zeros_like(key_sum)
        value_sum[...] = jnp.zeros_like(value_sum)

        def block(step, carry):
            at = pl.multiple_of(step * TOKEN_BLOCK, TOKEN_BLOCK)
            tokens = pl.ds(group * group_len + at, TOKEN_BLOCK)
            made = []
            for cols in heads:
                q = queries[tokens, cols]
                dout = upstream[tokens, cols]
                scores = lax.dot_general(keys[rows, cols], q, ONES, preferred_element_type=F32)
                dprob = lax.dot_general(values[rows, cols], dout, ONES, preferred_element_type=F32)
                made.append((cols, q, dout, scores, dprob))
            for cols, q, dout, scores, dprob in made:
                top = jnp.max(scores, axis=0, keepdims=True)
                powers = jnp.exp2((scores - top) * sharpness)
                probs = powers * (1.0 / jnp.sum(powers, axis=0, keepdims=True))
                delta = jnp.sum(probs * dprob, axis=0, keepdims=True)
                dscore = (probs * (dprob - delta)).astype(BF16)
                key_sum[:, cols] += jnp.dot(dscore, q, preferred_element_type=F32)
                value_sum[:, cols] += jnp.dot(probs.astype(BF16), dout, preferred_element_type=F32)
                grad = lax.dot_general(dscore, keys[rows, cols], ZEROS, preferred_element_type=F32)
                query_grad[tokens, cols] = (grad * scale).astype(BF16)
            return carry

        lax.fori_loop(0, blocks, block, 0)

        def blank(step, carry):
            tokens = pl.ds(group * group_len + pl.multiple_of(step * TOKEN_BLOCK, TOKEN_BLOCK), TOKEN_BLOCK)
            query_grad[tokens, :] = jnp.zeros((TOKEN_BLOCK, PAIR), BF16)
            return carry

        lax.fori_loop(blocks, group_len // TOKEN_BLOCK, blank, 0)
        key_part[rows, :] = (key_sum[...] * scale).astype(BF16)
        value_part[rows, :] = value_sum[...].astype(BF16)

    quarter = picked_t.shape[0] // SIDE
    for major in range(SIDE):
        rows = slice(major * quarter, (major + 1) * quarter)
        for part in (key_part, value_part):
            product = jnp.dot(picked_t[rows, :], part[...], preferred_element_type=F32)
            yield major, part is value_part, product.astype(BF16)


def stage_kernel(groups, named, numbers, gate_tanh, key_weight, value_weight, queries, upstream, *refs):
    key_out, value_out, queries_out, dout, numbers_out, raw, copied, arrived = refs
    tokens = upstream.shape[0]
    lengths_at = numbers_at(groups, named, SIDE * SIDE)[1]
    moves = [
        pltpu.make_async_copy(source, target, copied.at[at])
        for at, (source, target) in enumerate(
            ((key_weight, key_out), (value_weight, value_out), (queries, queries_out))
        )
    ]
    chunk = tokens // arrived.shape[0]
    loads = [
        pltpu.make_async_copy(upstream.at[pl.ds(at * chunk, chunk)], raw.at[pl.ds(at * chunk, chunk)], arrived.at[at])
        for at in range(arrived.shape[0])
    ]
    for move in loads + moves:
        move.start()
    for at, load in enumerate(loads):
        load.wait()
        group, first = divmod(at * chunk, tokens // groups)
        rows = slice(at * chunk, (at + 1) * chunk)
        live = lax.broadcasted_iota(jnp.int32, (chunk, upstream.shape[1]), 0) + first < numbers[lengths_at + group]
        dout[rows, :] = jnp.where(live, gate_tanh[...] * raw[rows, :].astype(F32), 0.0).astype(BF16)
    for move in moves:
        move.wait()
    for at in range(numbers.shape[0]):
        numbers_out[at] = numbers[at]


def stage(numbers, gate_tanh, key_weight, value_weight, queries, upstream, groups, named):
    arrays = [pltpu.with_memory_space_constraint(a, pltpu.HBM) for a in (key_weight, value_weight, queries, upstream)]
    return pl.pallas_call(
        functools.partial(stage_kernel, groups, named),
        in_specs=[pl.BlockSpec(memory_space=pltpu.SMEM), pl.BlockSpec(memory_space=pltpu.VMEM)]
        + [pl.BlockSpec(memory_space=pltpu.HBM)] * 4,
        out_specs=[pl.BlockSpec(memory_space=pltpu.VMEM)] * 4 + [pl.BlockSpec(memory_space=pltpu.SMEM)],
        out_shape=[pltpu.VMEM(array.shape, array.dtype) for array in arrays] + [jax.ShapeDtypeStruct(numbers.shape, numbers.dtype)],
        scratch_shapes=[
            pltpu.VMEM(upstream.shape, BF16),
            pltpu.SemaphoreType.DMA((3,)),
            pltpu.SemaphoreType.DMA((8,)),
        ],
        compiler_params=pltpu.CompilerParams(vmem_limit_bytes=24 * 1024 * 1024),
        cost_estimate=pl.CostEstimate(flops=10**7, bytes_accessed=2 * 10**7, transcendentals=0),
    )(numbers, gate_tanh, *arrays)


def first_kernel(groups, named, numbers, *refs):
    parts, (key_weight, value_weight, queries, upstream) = refs[:8], refs[8:12]
    query_grad, messages, (picked, picked_t), turned, scratch = refs[12], refs[13:17], refs[17:19], refs[19], refs[20:]

    @pl.when(pl.program_id(0) == 0)
    def _():
        pick(numbers, parts, picked, turned, picked_t, groups, named)

    share = picked.shape[1] // (SIDE * SIDE)
    for major, second, product in backward(
        numbers, picked, picked_t, key_weight, value_weight, queries, upstream, query_grad, scratch, groups, named
    ):
        for minor in range(SIDE):
            to = (2 * minor + second) * share
            messages[major][to : to + share, :] = product[minor * share : (minor + 1) * share]


def second_kernel(groups, named, numbers, *refs):
    picked, picked_t, key_weight, value_weight, queries, upstream = refs[:6]
    query_grad, messages, scratch = refs[7], refs[8:16], refs[16:]
    for major, second, product in backward(
        numbers, picked, picked_t, key_weight, value_weight, queries, upstream, query_grad, scratch, groups, named
    ):
        messages[second * SIDE + major][...] = product


def attention(numbers, latents, key_weight, value_weight, queries, upstream, query_grad, groups, named):
    first = query_grad is None
    tokens, width = queries.shape
    vision = key_weight.shape[0]
    steps = width // PAIR // 2
    offset = 0 if first else steps
    picked_rows = groups * named * LATENTS
    group_keys = named * LATENTS
    quarter = vision // SIDE
    whole = lambda shape: pl.BlockSpec(shape, lambda step, *_: (0, 0), pipeline_mode=pl.Buffered(1))
    columns = lambda rows: pl.BlockSpec((rows, PAIR), lambda step, *_: (0, step + offset))
    message = lambda rows: pl.BlockSpec((rows, PAIR), lambda step, *_: (0, step))
    shape = jax.ShapeDtypeStruct
    in_specs = [whole(part.shape) for part in latents]
    in_specs += [columns(vision), columns(vision), columns(tokens), columns(tokens)]
    inputs = [numbers, *latents, key_weight, value_weight, queries, upstream]
    out_specs, out_shape = [columns(tokens)], [shape((tokens, width), BF16)]
    scratch = [
        pltpu.VMEM((picked_rows, PAIR), BF16),
        pltpu.VMEM((picked_rows, PAIR), BF16),
        pltpu.VMEM((group_keys, PAIR), F32),
        pltpu.VMEM((group_keys, PAIR), F32),
        pltpu.VMEM((picked_rows, PAIR), BF16),
        pltpu.VMEM((picked_rows, PAIR), BF16),
    ]
    if first:
        out_specs += [message(2 * quarter)] * SIDE + [whole((picked_rows, vision)), whole((vision, picked_rows))]
        out_shape += [shape((2 * quarter, width // 2), BF16)] * SIDE
        out_shape += [shape((picked_rows, vision), BF16), shape((vision, picked_rows), BF16)]
        scratch = [pltpu.VMEM((vision, picked_rows), BF16)] + scratch
        aliases = {}
    else:
        in_specs.append(pl.BlockSpec(memory_space=pl.ANY))
        inputs.append(query_grad)
        out_specs += [message(quarter)] * (2 * SIDE)
        out_shape += [shape((quarter, width // 2), BF16)] * (2 * SIDE)
        aliases = {len(inputs) - 1: 0}
    return pl.pallas_call(
        functools.partial(first_kernel if first else second_kernel, groups, named),
        grid_spec=pltpu.PrefetchScalarGridSpec(
            num_scalar_prefetch=1, grid=(steps,), in_specs=in_specs, out_specs=out_specs, scratch_shapes=scratch
        ),
        out_shape=out_shape,
        input_output_aliases=aliases,
        compiler_params=pltpu.CompilerParams(vmem_limit_bytes=28 * 1024 * 1024),
        cost_estimate=pl.CostEstimate(flops=10**10, bytes_accessed=10**7, transcendentals=0),
    )(*inputs)


def add(*arrays):
    return functools.reduce(jnp.add, [array.astype(F32) for array in arrays])


def last_sum(shares, mp):
    came = [shift(shares[at].astype(BF16), 0, at, mp) for at in (2, 1, 3)]
    total = add(shares[0], *came)
    rows = total.shape[0] // 2
    return total[:rows], total[rows:]


def local(latents, key_weight, value_weight, queries, upstream, gate, media, frame_slot, lengths, *, mp):
    groups, named = media.shape
    place = jnp.stack([lax.axis_index("seq"), lax.axis_index("mp") % 2]).astype(jnp.int32)
    numbers = jnp.concatenate([media.reshape(-1), frame_slot, lengths, place])
    arrays = (key_weight, value_weight, queries, upstream)
    parts, numbers, rest = gather_latents(latents, numbers, jnp.tanh(gate)[None, :], arrays, groups, named, mp)
    query_grad, *joined, picked, picked_t = attention(numbers, parts, *rest, None, groups, named)
    came = [shift(joined[at], at, 0, mp) for at in (2, 1, 3)]

    query_grad, *messages = attention(numbers, (picked, picked_t), *rest, query_grad, groups, named)
    rows, messages = lax.optimization_barrier((add(joined[0], *came), messages))
    key, value = messages[:SIDE], messages[SIDE:]
    key_far = shift(key[2], 1, 0, mp)
    value_far = shift(value[2], 3, 0, mp)
    value_near = shift(value[1], 1, 0, mp)
    key_near = shift(key[3], 3, 0, mp)

    share = rows.shape[0] // SIDE
    first = last_sum([rows[at * share : (at + 1) * share] for at in range(SIDE)], mp)

    key_on = shift(add(key[1], key_far).astype(BF16), 1, 0, mp)
    value_on = shift(add(value[3], value_far).astype(BF16), 3, 0, mp)
    key_rows = add(key[0], key_near, key_on)
    value_rows = add(value[0], value_near, value_on)
    share //= 2
    cut = lambda array, at: array[at * share : (at + 1) * share]
    second = last_sum([jnp.concatenate([cut(key_rows, at), cut(value_rows, at)], axis=0) for at in range(SIDE)], mp)
    key_grad, value_grad = [jnp.concatenate(halves, axis=1) for halves in zip(first, second)]
    return query_grad, key_grad, value_grad


def solution(mesh):
    in_specs = (
        P("seq", None),
        P(None, "mp"),
        P(None, "mp"),
        P("seq", "mp"),
        P("seq", "mp"),
        P("mp"),
        P("seq", None),
        P(),
        P("seq"),
    )
    out_specs = (P("seq", "mp"), P("seq", "mp"), P("seq", "mp"))
    body = functools.partial(local, mp=mesh.shape["mp"])
    return jax.shard_map(body, mesh=mesh, in_specs=in_specs, out_specs=out_specs, check_vma=False)
```

```python
import functools
import math

import jax
import jax.numpy as jnp
from jax import lax
from jax.experimental import pallas as pl
from jax.experimental.pallas import tpu as pltpu
from jax.sharding import PartitionSpec as P

HEAD_DIM = 128
LATENTS = 64
SIDE = 4
HEADS = 4
PAIR = HEADS * HEAD_DIM
TOKEN_BLOCK = 256
ONES = (((1,), (1,)), ((), ()))
ZEROS = (((0,), (0,)), ((), ()))
BF16 = jnp.bfloat16
F32 = jnp.float32


def shift(array, major, minor, mp):
    pairs = []
    for x in range(SIDE):
        for z in range(SIDE):
            for m in range(mp):
                dx, dz = (major, minor) if m % 2 == 0 else (minor, major)
                to = ((x + dx) % SIDE) * SIDE + (z + dz) % SIDE
                pairs.append(((x * SIDE + z) * mp + m, to * mp + m))
    return lax.ppermute(array, ("seq", "mp"), pairs)


def swap_cores(array, mp):
    return lax.ppermute(array, "mp", [(m, m ^ 1) for m in range(mp)])


def gather_latents(latents, numbers, gate_tanh, arrays, groups, named, mp):
    half = latents.shape[1] // 2
    mine = jnp.where(lax.axis_index("mp") % 2 == 0, latents[:, :half], latents[:, half:])
    far = shift(mine, 2, 0, mp)
    near = [shift(mine, step, 0, mp) for step in (1, 3)]
    line = jnp.concatenate([mine, near[0], far, near[1]], axis=0)
    line, numbers, gate_tanh = lax.optimization_barrier((line, numbers, gate_tanh))
    far = shift(line, 0, 2, mp)
    near = [shift(line, 0, step, mp) for step in (1, 3)]
    *arrays, numbers = stage(numbers, gate_tanh, *arrays, groups, named)
    *fetched, numbers = lax.optimization_barrier((line, near[0], far, near[1], numbers))
    return fetched + [swap_cores(part, mp) for part in fetched], numbers, arrays


def numbers_at(groups, named, frames):
    slots = groups * named
    lengths = slots + frames
    return slots, lengths, lengths + groups


def pick(numbers, parts, picked, turned, picked_t, groups, named):
    slots_at, lengths_at, place_at = numbers_at(groups, named, SIDE * SIDE)
    half = parts[0].shape[1]
    seq, core = numbers[place_at], numbers[place_at + 1]
    x, z = seq // SIDE, seq % SIDE
    for name in range(groups * named):
        slot = numbers[slots_at + numbers[name]]
        dx = (x - slot // SIDE + SIDE) % SIDE
        dz = (z - slot % SIDE + SIDE) % SIDE
        to = pl.ds(name * LATENTS, LATENTS)
        for side in range(2):
            minor, major = (dx, dz) if side == 0 else (dz, dx)
            start = pl.ds(pl.multiple_of(minor * LATENTS, LATENTS), LATENTS)
            first = jnp.where(core == side, 0, 4)
            for at in range(8):

                @pl.when(first + major == at)
                def _():
                    picked[to, side * half : (side + 1) * half] = parts[at][start, :]

    turned[...] = picked[...].T
    share = turned.shape[0] // (SIDE * SIDE)
    for major in range(SIDE):
        for minor in range(SIDE):
            dx = jnp.where(core == 0, major, minor)
            dz = jnp.where(core == 0, minor, major)
            owner = ((x + dx) % SIDE) * SIDE + (z + dz) % SIDE
            to = (major * SIDE + minor) * share
            picked_t[to : to + share, :] = turned[pl.ds(pl.multiple_of(owner * share, 16), share), :]


def backward(numbers, picked, picked_t, key_weight, value_weight, queries, upstream, query_grad, scratch, groups, named):
    keys, values, key_sum, value_sum, key_part, value_part = scratch
    lengths_at = numbers_at(groups, named, SIDE * SIDE)[1]
    group_keys = named * LATENTS
    group_len = queries.shape[0] // groups
    scale = HEAD_DIM**-0.5
    sharpness = scale * math.log2(math.e)
    keys[...] = jnp.dot(picked[...], key_weight[...], preferred_element_type=F32).astype(BF16)
    values[...] = jnp.dot(picked[...], value_weight[...], preferred_element_type=F32).astype(BF16)
    heads = [slice(head * HEAD_DIM, (head + 1) * HEAD_DIM) for head in range(HEADS)]

    for group in range(groups):
        rows = slice(group * group_keys, (group + 1) * group_keys)
        length = numbers[lengths_at + group]
        blocks = (length + TOKEN_BLOCK - 1) // TOKEN_BLOCK
        key_sum[...] = jnp.zeros_like(key_sum)
        value_sum[...] = jnp.zeros_like(value_sum)

        def block(step, carry):
            at = pl.multiple_of(step * TOKEN_BLOCK, TOKEN_BLOCK)
            tokens = pl.ds(group * group_len + at, TOKEN_BLOCK)
            made = []
            for cols in heads:
                q = queries[tokens, cols]
                dout = upstream[tokens, cols]
                scores = lax.dot_general(keys[rows, cols], q, ONES, preferred_element_type=F32)
                dprob = lax.dot_general(values[rows, cols], dout, ONES, preferred_element_type=F32)
                made.append((cols, q, dout, scores, dprob))
            for cols, q, dout, scores, dprob in made:
                top = jnp.max(scores, axis=0, keepdims=True)
                powers = jnp.exp2((scores - top) * sharpness)
                probs = powers * (1.0 / jnp.sum(powers, axis=0, keepdims=True))
                delta = jnp.sum(probs * dprob, axis=0, keepdims=True)
                dscore = (probs * (dprob - delta)).astype(BF16)
                key_sum[:, cols] += jnp.dot(dscore, q, preferred_element_type=F32)
                value_sum[:, cols] += jnp.dot(probs.astype(BF16), dout, preferred_element_type=F32)
                grad = lax.dot_general(dscore, keys[rows, cols], ZEROS, preferred_element_type=F32)
                query_grad[tokens, cols] = (grad * scale).astype(BF16)
            return carry

        lax.fori_loop(0, blocks, block, 0)

        def blank(step, carry):
            tokens = pl.ds(group * group_len + pl.multiple_of(step * TOKEN_BLOCK, TOKEN_BLOCK), TOKEN_BLOCK)
            query_grad[tokens, :] = jnp.zeros((TOKEN_BLOCK, PAIR), BF16)
            return carry

        lax.fori_loop(blocks, group_len // TOKEN_BLOCK, blank, 0)
        key_part[rows, :] = (key_sum[...] * scale).astype(BF16)
        value_part[rows, :] = value_sum[...].astype(BF16)

    quarter = picked_t.shape[0] // SIDE
    for major in range(SIDE):
        rows = slice(major * quarter, (major + 1) * quarter)
        for part in (key_part, value_part):
            product = jnp.dot(picked_t[rows, :], part[...], preferred_element_type=F32)
            yield major, part is value_part, product.astype(BF16)


def stage_kernel(groups, named, numbers, gate_tanh, key_weight, value_weight, queries, upstream, *refs):
    key_out, value_out, queries_out, dout, numbers_out, raw, copied, arrived = refs
    tokens = upstream.shape[0]
    lengths_at = numbers_at(groups, named, SIDE * SIDE)[1]
    moves = [
        pltpu.make_async_copy(source, target, copied.at[at])
        for at, (source, target) in enumerate(
            ((key_weight, key_out), (value_weight, value_out), (queries, queries_out))
        )
    ]
    chunk = tokens // arrived.shape[0]
    loads = [
        pltpu.make_async_copy(upstream.at[pl.ds(at * chunk, chunk)], raw.at[pl.ds(at * chunk, chunk)], arrived.at[at])
        for at in range(arrived.shape[0])
    ]
    for move in loads + moves:
        move.start()
    for at, load in enumerate(loads):
        load.wait()
        group, first = divmod(at * chunk, tokens // groups)
        rows = slice(at * chunk, (at + 1) * chunk)
        live = lax.broadcasted_iota(jnp.int32, (chunk, upstream.shape[1]), 0) + first < numbers[lengths_at + group]
        dout[rows, :] = jnp.where(live, gate_tanh[...] * raw[rows, :].astype(F32), 0.0).astype(BF16)
    for move in moves:
        move.wait()
    for at in range(numbers.shape[0]):
        numbers_out[at] = numbers[at]


def stage(numbers, gate_tanh, key_weight, value_weight, queries, upstream, groups, named):
    arrays = [pltpu.with_memory_space_constraint(a, pltpu.HBM) for a in (key_weight, value_weight, queries, upstream)]
    return pl.pallas_call(
        functools.partial(stage_kernel, groups, named),
        in_specs=[pl.BlockSpec(memory_space=pltpu.SMEM), pl.BlockSpec(memory_space=pltpu.VMEM)]
        + [pl.BlockSpec(memory_space=pltpu.HBM)] * 4,
        out_specs=[pl.BlockSpec(memory_space=pltpu.VMEM)] * 4 + [pl.BlockSpec(memory_space=pltpu.SMEM)],
        out_shape=[pltpu.VMEM(array.shape, array.dtype) for array in arrays] + [jax.ShapeDtypeStruct(numbers.shape, numbers.dtype)],
        scratch_shapes=[
            pltpu.VMEM(upstream.shape, BF16),
            pltpu.SemaphoreType.DMA((3,)),
            pltpu.SemaphoreType.DMA((8,)),
        ],
        compiler_params=pltpu.CompilerParams(vmem_limit_bytes=24 * 1024 * 1024),
        cost_estimate=pl.CostEstimate(flops=10**7, bytes_accessed=2 * 10**7, transcendentals=0),
    )(numbers, gate_tanh, *arrays)


def first_kernel(groups, named, numbers, *refs):
    parts, staged = refs[:8], [ref.at[:, :PAIR] for ref in refs[8:12]]
    query_grad, messages, (picked, picked_t), turned, scratch = refs[12], refs[13:17], refs[17:19], refs[19], refs[20:]

    @pl.when(pl.program_id(0) == 0)
    def _():
        pick(numbers, parts, picked, turned, picked_t, groups, named)

    share = picked.shape[1] // (SIDE * SIDE)
    for major, second, product in backward(
        numbers, picked, picked_t, *staged, query_grad, scratch, groups, named
    ):
        for minor in range(SIDE):
            to = (2 * minor + second) * share
            messages[major][to : to + share, :] = product[minor * share : (minor + 1) * share]


def second_kernel(groups, named, numbers, *refs):
    picked, picked_t, *staged = refs[:2] + tuple(ref.at[:, PAIR:] for ref in refs[2:6])
    query_grad, messages, scratch = refs[7], refs[8:16], refs[16:]
    for major, second, product in backward(
        numbers, picked, picked_t, *staged, query_grad, scratch, groups, named
    ):
        messages[second * SIDE + major][...] = product


def attention(numbers, latents, key_weight, value_weight, queries, upstream, query_grad, groups, named):
    first = query_grad is None
    tokens, width = queries.shape
    vision = key_weight.shape[0]
    steps = width // PAIR // 2
    offset = 0 if first else steps
    picked_rows = groups * named * LATENTS
    group_keys = named * LATENTS
    quarter = vision // SIDE
    whole = lambda shape: pl.BlockSpec(shape, lambda step, *_: (0, 0), pipeline_mode=pl.Buffered(1))
    columns = lambda rows: pl.BlockSpec((rows, PAIR), lambda step, *_: (0, step + offset))
    message = lambda rows: pl.BlockSpec((rows, PAIR), lambda step, *_: (0, step))
    shape = jax.ShapeDtypeStruct
    in_specs = [whole(part.shape) for part in latents]
    in_specs += [pl.BlockSpec(memory_space=pltpu.VMEM)] * 4
    staged = [pltpu.with_memory_space_constraint(array, pltpu.VMEM) for array in (key_weight, value_weight, queries, upstream)]
    inputs = [numbers, *latents, *staged]
    out_specs, out_shape = [columns(tokens)], [shape((tokens, width), BF16)]
    scratch = [
        pltpu.VMEM((picked_rows, PAIR), BF16),
        pltpu.VMEM((picked_rows, PAIR), BF16),
        pltpu.VMEM((group_keys, PAIR), F32),
        pltpu.VMEM((group_keys, PAIR), F32),
        pltpu.VMEM((picked_rows, PAIR), BF16),
        pltpu.VMEM((picked_rows, PAIR), BF16),
    ]
    if first:
        out_specs += [message(2 * quarter)] * SIDE + [whole((picked_rows, vision)), whole((vision, picked_rows))]
        out_shape += [shape((2 * quarter, width // 2), BF16)] * SIDE
        out_shape += [shape((picked_rows, vision), BF16), shape((vision, picked_rows), BF16)]
        scratch = [pltpu.VMEM((vision, picked_rows), BF16)] + scratch
        aliases = {}
    else:
        in_specs.append(pl.BlockSpec(memory_space=pl.ANY))
        inputs.append(query_grad)
        out_specs += [message(quarter)] * (2 * SIDE)
        out_shape += [shape((quarter, width // 2), BF16)] * (2 * SIDE)
        aliases = {len(inputs) - 1: 0}
    return pl.pallas_call(
        functools.partial(first_kernel if first else second_kernel, groups, named),
        grid_spec=pltpu.PrefetchScalarGridSpec(
            num_scalar_prefetch=1, grid=(steps,), in_specs=in_specs, out_specs=out_specs, scratch_shapes=scratch
        ),
        out_shape=out_shape,
        input_output_aliases=aliases,
        compiler_params=pltpu.CompilerParams(vmem_limit_bytes=28 * 1024 * 1024),
        cost_estimate=pl.CostEstimate(flops=10**10, bytes_accessed=10**7, transcendentals=0),
    )(*inputs)


def add(*arrays):
    return functools.reduce(jnp.add, [array.astype(F32) for array in arrays])


def last_sum(shares, mp):
    came = [shift(shares[at].astype(BF16), 0, at, mp) for at in (2, 1, 3)]
    total = add(shares[0], *came)
    rows = total.shape[0] // 2
    return total[:rows], total[rows:]


def local(latents, key_weight, value_weight, queries, upstream, gate, media, frame_slot, lengths, *, mp):
    groups, named = media.shape
    place = jnp.stack([lax.axis_index("seq"), lax.axis_index("mp") % 2]).astype(jnp.int32)
    numbers = jnp.concatenate([media.reshape(-1), frame_slot, lengths, place])
    arrays = (key_weight, value_weight, queries, upstream)
    parts, numbers, rest = gather_latents(latents, numbers, jnp.tanh(gate)[None, :], arrays, groups, named, mp)
    query_grad, *joined, picked, picked_t = attention(numbers, parts, *rest, None, groups, named)
    came = [shift(joined[at], at, 0, mp) for at in (2, 1, 3)]

    query_grad, *messages = attention(numbers, (picked, picked_t), *rest, query_grad, groups, named)
    rows, messages = lax.optimization_barrier((add(joined[0], *came), messages))
    key, value = messages[:SIDE], messages[SIDE:]
    key_far = shift(key[2], 1, 0, mp)
    value_far = shift(value[2], 3, 0, mp)
    value_near = shift(value[1], 1, 0, mp)
    key_near = shift(key[3], 3, 0, mp)

    share = rows.shape[0] // SIDE
    first = last_sum([rows[at * share : (at + 1) * share] for at in range(SIDE)], mp)

    key_on = shift(add(key[1], key_far).astype(BF16), 1, 0, mp)
    value_on = shift(add(value[3], value_far).astype(BF16), 3, 0, mp)
    key_rows = add(key[0], key_near, key_on)
    value_rows = add(value[0], value_near, value_on)
    share //= 2
    cut = lambda array, at: array[at * share : (at + 1) * share]
    second = last_sum([jnp.concatenate([cut(key_rows, at), cut(value_rows, at)], axis=0) for at in range(SIDE)], mp)
    key_grad, value_grad = [jnp.concatenate(halves, axis=1) for halves in zip(first, second)]
    return query_grad, key_grad, value_grad


def solution(mesh):
    in_specs = (
        P("seq", None),
        P(None, "mp"),
        P(None, "mp"),
        P("seq", "mp"),
        P("seq", "mp"),
        P("mp"),
        P("seq", None),
        P(),
        P("seq"),
    )
    out_specs = (P("seq", "mp"), P("seq", "mp"), P("seq", "mp"))
    body = functools.partial(local, mp=mesh.shape["mp"])
    return jax.shard_map(body, mesh=mesh, in_specs=in_specs, out_specs=out_specs, check_vma=False)
```

```python
import functools
import math

import jax
import jax.numpy as jnp
from jax import lax
from jax.experimental import pallas as pl
from jax.experimental.pallas import tpu as pltpu
from jax.sharding import PartitionSpec as P

HEAD_DIM = 128
LATENTS = 64
SIDE = 4
HEADS = 4
PAIR = HEADS * HEAD_DIM
TOKEN_BLOCK = 256
ONES = (((1,), (1,)), ((), ()))
ZEROS = (((0,), (0,)), ((), ()))
BF16 = jnp.bfloat16
F32 = jnp.float32


def shift(array, major, minor, mp):
    pairs = []
    for x in range(SIDE):
        for z in range(SIDE):
            for m in range(mp):
                dx, dz = (major, minor) if m % 2 == 0 else (minor, major)
                to = ((x + dx) % SIDE) * SIDE + (z + dz) % SIDE
                pairs.append(((x * SIDE + z) * mp + m, to * mp + m))
    return lax.ppermute(array, ("seq", "mp"), pairs)


def swap_cores(array, mp):
    return lax.ppermute(array, "mp", [(m, m ^ 1) for m in range(mp)])


def gather_latents(latents, numbers, gate_tanh, arrays, groups, named, mp):
    half = latents.shape[1] // 2
    mine = jnp.where(lax.axis_index("mp") % 2 == 0, latents[:, :half], latents[:, half:])
    far = shift(mine, 2, 0, mp)
    near = [shift(mine, step, 0, mp) for step in (1, 3)]
    line = jnp.concatenate([mine, near[0], far, near[1]], axis=0)
    line, numbers, gate_tanh = lax.optimization_barrier((line, numbers, gate_tanh))
    far = shift(line, 0, 2, mp)
    near = [shift(line, 0, step, mp) for step in (1, 3)]
    *arrays, numbers = stage(numbers, gate_tanh, *arrays, groups, named)
    *fetched, numbers = lax.optimization_barrier((line, near[0], far, near[1], numbers))
    return fetched + [swap_cores(part, mp) for part in fetched], numbers, arrays


def numbers_at(groups, named, frames):
    slots = groups * named
    lengths = slots + frames
    return slots, lengths, lengths + groups


def pick(numbers, parts, picked, turned, picked_t, groups, named):
    slots_at, lengths_at, place_at = numbers_at(groups, named, SIDE * SIDE)
    half = parts[0].shape[1]
    seq, core = numbers[place_at], numbers[place_at + 1]
    x, z = seq // SIDE, seq % SIDE
    for name in range(groups * named):
        slot = numbers[slots_at + numbers[name]]
        dx = (x - slot // SIDE + SIDE) % SIDE
        dz = (z - slot % SIDE + SIDE) % SIDE
        to = pl.ds(name * LATENTS, LATENTS)
        for side in range(2):
            minor, major = (dx, dz) if side == 0 else (dz, dx)
            start = pl.ds(pl.multiple_of(minor * LATENTS, LATENTS), LATENTS)
            first = jnp.where(core == side, 0, 4)
            for at in range(8):

                @pl.when(first + major == at)
                def _():
                    picked[to, side * half : (side + 1) * half] = parts[at][start, :]

    turned[...] = picked[...].T
    share = turned.shape[0] // (SIDE * SIDE)
    for major in range(SIDE):
        for minor in range(SIDE):
            dx = jnp.where(core == 0, major, minor)
            dz = jnp.where(core == 0, minor, major)
            owner = ((x + dx) % SIDE) * SIDE + (z + dz) % SIDE
            to = (major * SIDE + minor) * share
            picked_t[to : to + share, :] = turned[pl.ds(pl.multiple_of(owner * share, 16), share), :]


def backward(numbers, picked, picked_t, key_weight, value_weight, queries, upstream, query_grad, scratch, groups, named):
    keys, values, key_sum, value_sum, key_part, value_part = scratch
    lengths_at = numbers_at(groups, named, SIDE * SIDE)[1]
    group_keys = named * LATENTS
    group_len = queries.shape[0] // groups
    scale = HEAD_DIM**-0.5
    sharpness = scale * math.log2(math.e)
    keys[...] = jnp.dot(picked[...], key_weight[...], preferred_element_type=F32).astype(BF16)
    values[...] = jnp.dot(picked[...], value_weight[...], preferred_element_type=F32).astype(BF16)
    heads = [slice(head * HEAD_DIM, (head + 1) * HEAD_DIM) for head in range(HEADS)]

    for group in range(groups):
        rows = slice(group * group_keys, (group + 1) * group_keys)
        length = numbers[lengths_at + group]
        blocks = (length + TOKEN_BLOCK - 1) // TOKEN_BLOCK
        key_sum[...] = jnp.zeros_like(key_sum)
        value_sum[...] = jnp.zeros_like(value_sum)

        def block(step, carry):
            at = pl.multiple_of(step * TOKEN_BLOCK, TOKEN_BLOCK)
            tokens = pl.ds(group * group_len + at, TOKEN_BLOCK)
            made = []
            for cols in heads:
                q = queries[tokens, cols]
                dout = upstream[tokens, cols]
                scores = lax.dot_general(keys[rows, cols], q, ONES, preferred_element_type=F32)
                dprob = lax.dot_general(values[rows, cols], dout, ONES, preferred_element_type=F32)
                made.append((cols, q, dout, scores, dprob))
            for cols, q, dout, scores, dprob in made:
                top = jnp.max(scores, axis=0, keepdims=True)
                powers = jnp.exp2((scores - top) * sharpness)
                probs = powers * (1.0 / jnp.sum(powers, axis=0, keepdims=True))
                delta = jnp.sum(probs * dprob, axis=0, keepdims=True)
                dscore = (probs * (dprob - delta)).astype(BF16)
                key_sum[:, cols] += jnp.dot(dscore, q, preferred_element_type=F32)
                value_sum[:, cols] += jnp.dot(probs.astype(BF16), dout, preferred_element_type=F32)
                grad = lax.dot_general(dscore, keys[rows, cols], ZEROS, preferred_element_type=F32)
                query_grad[tokens, cols] = (grad * scale).astype(BF16)
            return carry

        lax.fori_loop(0, blocks, block, 0)

        def blank(step, carry):
            tokens = pl.ds(group * group_len + pl.multiple_of(step * TOKEN_BLOCK, TOKEN_BLOCK), TOKEN_BLOCK)
            query_grad[tokens, :] = jnp.zeros((TOKEN_BLOCK, PAIR), BF16)
            return carry

        lax.fori_loop(blocks, group_len // TOKEN_BLOCK, blank, 0)
        key_part[rows, :] = (key_sum[...] * scale).astype(BF16)
        value_part[rows, :] = value_sum[...].astype(BF16)

    quarter = picked_t.shape[0] // SIDE
    for major in range(SIDE):
        rows = slice(major * quarter, (major + 1) * quarter)
        for part in (key_part, value_part):
            product = jnp.dot(picked_t[rows, :], part[...], preferred_element_type=F32)
            yield major, part is value_part, product.astype(BF16)


def stage_kernel(groups, named, numbers, gate_tanh, key_weight, value_weight, queries, upstream, *refs):
    key_out, value_out, queries_out, dout, numbers_out, raw, copied, arrived = refs
    tokens = upstream.shape[0]
    lengths_at = numbers_at(groups, named, SIDE * SIDE)[1]
    moves = [
        pltpu.make_async_copy(source, target, copied.at[at])
        for at, (source, target) in enumerate(
            ((key_weight, key_out), (value_weight, value_out), (queries, queries_out))
        )
    ]
    chunk = tokens // arrived.shape[0]
    loads = [
        pltpu.make_async_copy(upstream.at[pl.ds(at * chunk, chunk)], raw.at[pl.ds(at * chunk, chunk)], arrived.at[at])
        for at in range(arrived.shape[0])
    ]
    for move in loads + moves:
        move.start()
    for at, load in enumerate(loads):
        load.wait()
        group, first = divmod(at * chunk, tokens // groups)
        rows = slice(at * chunk, (at + 1) * chunk)
        live = lax.broadcasted_iota(jnp.int32, (chunk, upstream.shape[1]), 0) + first < numbers[lengths_at + group]
        dout[rows, :] = jnp.where(live, gate_tanh[...] * raw[rows, :].astype(F32), 0.0).astype(BF16)
    for move in moves:
        move.wait()
    for at in range(numbers.shape[0]):
        numbers_out[at] = numbers[at]


def stage(numbers, gate_tanh, key_weight, value_weight, queries, upstream, groups, named):
    arrays = [pltpu.with_memory_space_constraint(a, pltpu.HBM) for a in (key_weight, value_weight, queries, upstream)]
    return pl.pallas_call(
        functools.partial(stage_kernel, groups, named),
        in_specs=[pl.BlockSpec(memory_space=pltpu.SMEM), pl.BlockSpec(memory_space=pltpu.VMEM)]
        + [pl.BlockSpec(memory_space=pltpu.HBM)] * 4,
        out_specs=[pl.BlockSpec(memory_space=pltpu.VMEM)] * 4 + [pl.BlockSpec(memory_space=pltpu.SMEM)],
        out_shape=[pltpu.VMEM(array.shape, array.dtype) for array in arrays] + [jax.ShapeDtypeStruct(numbers.shape, numbers.dtype)],
        scratch_shapes=[
            pltpu.VMEM(upstream.shape, BF16),
            pltpu.SemaphoreType.DMA((3,)),
            pltpu.SemaphoreType.DMA((8,)),
        ],
        compiler_params=pltpu.CompilerParams(vmem_limit_bytes=24 * 1024 * 1024),
        cost_estimate=pl.CostEstimate(flops=10**7, bytes_accessed=2 * 10**7, transcendentals=0),
    )(numbers, gate_tanh, *arrays)


def first_kernel(groups, named, numbers, *refs):
    parts, staged = refs[:8], [ref.at[:, :PAIR] for ref in refs[8:12]]
    query_grad, messages, (picked, picked_t), turned, scratch = refs[12], refs[13:17], refs[17:19], refs[19], refs[20:]

    @pl.when(pl.program_id(0) == 0)
    def _():
        pick(numbers, parts, picked, turned, picked_t, groups, named)

    share = picked.shape[1] // (SIDE * SIDE)
    for major, second, product in backward(
        numbers, picked, picked_t, *staged, query_grad, scratch, groups, named
    ):
        for minor in range(SIDE):
            to = (2 * minor + second) * share
            messages[major][to : to + share, :] = product[minor * share : (minor + 1) * share]


def second_kernel(groups, named, numbers, *refs):
    picked, picked_t, *staged = refs[:2] + tuple(ref.at[:, PAIR:] for ref in refs[2:6])
    query_grad, messages, scratch = refs[7], refs[8:12], refs[12:]
    share = picked.shape[1] // (SIDE * SIDE)
    for major, second, product in backward(
        numbers, picked, picked_t, *staged, query_grad, scratch, groups, named
    ):
        for minor in range(SIDE):
            to = (2 * minor + second) * share
            messages[major][to : to + share, :] = product[minor * share : (minor + 1) * share]


def attention(numbers, latents, key_weight, value_weight, queries, upstream, query_grad, groups, named):
    first = query_grad is None
    tokens, width = queries.shape
    vision = key_weight.shape[0]
    steps = width // PAIR // 2
    offset = 0 if first else steps
    picked_rows = groups * named * LATENTS
    group_keys = named * LATENTS
    quarter = vision // SIDE
    whole = lambda shape: pl.BlockSpec(shape, lambda step, *_: (0, 0), pipeline_mode=pl.Buffered(1))
    columns = lambda rows: pl.BlockSpec((rows, PAIR), lambda step, *_: (0, step + offset))
    message = lambda rows: pl.BlockSpec((rows, PAIR), lambda step, *_: (0, step))
    shape = jax.ShapeDtypeStruct
    in_specs = [whole(part.shape) for part in latents]
    in_specs += [pl.BlockSpec(memory_space=pltpu.VMEM)] * 4
    staged = [pltpu.with_memory_space_constraint(array, pltpu.VMEM) for array in (key_weight, value_weight, queries, upstream)]
    inputs = [numbers, *latents, *staged]
    out_specs, out_shape = [columns(tokens)], [shape((tokens, width), BF16)]
    scratch = [
        pltpu.VMEM((picked_rows, PAIR), BF16),
        pltpu.VMEM((picked_rows, PAIR), BF16),
        pltpu.VMEM((group_keys, PAIR), F32),
        pltpu.VMEM((group_keys, PAIR), F32),
        pltpu.VMEM((picked_rows, PAIR), BF16),
        pltpu.VMEM((picked_rows, PAIR), BF16),
    ]
    if first:
        out_specs += [message(2 * quarter)] * SIDE + [whole((picked_rows, vision)), whole((vision, picked_rows))]
        out_shape += [shape((2 * quarter, width // 2), BF16)] * SIDE
        out_shape += [shape((picked_rows, vision), BF16), shape((vision, picked_rows), BF16)]
        scratch = [pltpu.VMEM((vision, picked_rows), BF16)] + scratch
        aliases = {}
    else:
        in_specs.append(pl.BlockSpec(memory_space=pl.ANY))
        inputs.append(query_grad)
        out_specs += [message(2 * quarter)] * SIDE
        out_shape += [shape((2 * quarter, width // 2), BF16)] * SIDE
        aliases = {len(inputs) - 1: 0}
    return pl.pallas_call(
        functools.partial(first_kernel if first else second_kernel, groups, named),
        grid_spec=pltpu.PrefetchScalarGridSpec(
            num_scalar_prefetch=1, grid=(steps,), in_specs=in_specs, out_specs=out_specs, scratch_shapes=scratch
        ),
        out_shape=out_shape,
        input_output_aliases=aliases,
        compiler_params=pltpu.CompilerParams(vmem_limit_bytes=28 * 1024 * 1024),
        cost_estimate=pl.CostEstimate(flops=10**10, bytes_accessed=10**7, transcendentals=0),
    )(*inputs)


def add(*arrays):
    return functools.reduce(jnp.add, [array.astype(F32) for array in arrays])


def last_hop(shares, mp):
    return [shares[0]] + [shift(shares[at].astype(BF16), 0, at, mp) for at in (2, 1, 3)]


def finish_kernel(*refs):
    *came, key_grad, value_grad = refs
    rows, width = key_grad.shape[0], key_grad.shape[1] // 2
    for at in range(2):
        total = functools.reduce(jnp.add, [ref[...].astype(F32) for ref in came[at * SIDE : (at + 1) * SIDE]])
        key_grad[:, at * width : (at + 1) * width] = total[:rows]
        value_grad[:, at * width : (at + 1) * width] = total[rows:]


def finish(first, second):
    rows, width = first[0].shape
    return pl.pallas_call(
        finish_kernel,
        out_shape=[jax.ShapeDtypeStruct((rows // 2, 2 * width), F32)] * 2,
        compiler_params=pltpu.CompilerParams(vmem_limit_bytes=8 * 1024 * 1024),
    )(*first, *second)


def local(latents, key_weight, value_weight, queries, upstream, gate, media, frame_slot, lengths, *, mp):
    groups, named = media.shape
    place = jnp.stack([lax.axis_index("seq"), lax.axis_index("mp") % 2]).astype(jnp.int32)
    numbers = jnp.concatenate([media.reshape(-1), frame_slot, lengths, place])
    arrays = (key_weight, value_weight, queries, upstream)
    parts, numbers, rest = gather_latents(latents, numbers, jnp.tanh(gate)[None, :], arrays, groups, named, mp)
    query_grad, *joined, picked, picked_t = attention(numbers, parts, *rest, None, groups, named)
    came = [shift(joined[at], at, 0, mp) for at in (2, 1, 3)]

    query_grad, *messages = attention(numbers, (picked, picked_t), *rest, query_grad, groups, named)
    rows, messages = lax.optimization_barrier((add(joined[0], *came), messages))
    came = [shift(messages[at], at, 0, mp) for at in (2, 1, 3)]
    share = rows.shape[0] // SIDE
    cut = lambda array: [array[at * share : (at + 1) * share] for at in range(SIDE)]
    first = last_hop(cut(rows), mp)
    second = last_hop(cut(add(messages[0], *came)), mp)
    key_grad, value_grad = finish(first, second)
    return query_grad, key_grad, value_grad


def solution(mesh):
    in_specs = (
        P("seq", None),
        P(None, "mp"),
        P(None, "mp"),
        P("seq", "mp"),
        P("seq", "mp"),
        P("mp"),
        P("seq", None),
        P(),
        P("seq"),
    )
    out_specs = (P("seq", "mp"), P("seq", "mp"), P("seq", "mp"))
    body = functools.partial(local, mp=mesh.shape["mp"])
    return jax.shard_map(body, mesh=mesh, in_specs=in_specs, out_specs=out_specs, check_vma=False)
```

```python
import functools
import math

import jax
import jax.numpy as jnp
from jax import lax
from jax.experimental import pallas as pl
from jax.experimental.pallas import tpu as pltpu
from jax.sharding import PartitionSpec as P

HEAD_DIM = 128
LATENTS = 64
SIDE = 4
HEADS = 4
PAIR = HEADS * HEAD_DIM
TOKEN_BLOCK = 512
ONES = (((1,), (1,)), ((), ()))
ZEROS = (((0,), (0,)), ((), ()))
BF16 = jnp.bfloat16
F32 = jnp.float32


def shift(array, major, minor, mp):
    pairs = []
    for x in range(SIDE):
        for z in range(SIDE):
            for m in range(mp):
                dx, dz = (major, minor) if m % 2 == 0 else (minor, major)
                to = ((x + dx) % SIDE) * SIDE + (z + dz) % SIDE
                pairs.append(((x * SIDE + z) * mp + m, to * mp + m))
    return lax.ppermute(array, ("seq", "mp"), pairs)


def swap_cores(array, mp):
    return lax.ppermute(array, "mp", [(m, m ^ 1) for m in range(mp)])


def gather_latents(latents, numbers, gate_tanh, arrays, groups, named, mp):
    half = latents.shape[1] // 2
    mine = jnp.where(lax.axis_index("mp") % 2 == 0, latents[:, :half], latents[:, half:])
    far = shift(mine, 2, 0, mp)
    near = [shift(mine, step, 0, mp) for step in (1, 3)]
    line = jnp.concatenate([mine, near[0], far, near[1]], axis=0)
    line, numbers, gate_tanh = lax.optimization_barrier((line, numbers, gate_tanh))
    far = shift(line, 0, 2, mp)
    near = [shift(line, 0, step, mp) for step in (1, 3)]
    *arrays, numbers = stage(numbers, gate_tanh, *arrays, groups, named)
    *fetched, numbers = lax.optimization_barrier((line, near[0], far, near[1], numbers))
    return fetched + [swap_cores(part, mp) for part in fetched], numbers, arrays


def numbers_at(groups, named, frames):
    slots = groups * named
    lengths = slots + frames
    return slots, lengths, lengths + groups


def pick(numbers, parts, picked, turned, picked_t, groups, named):
    slots_at, lengths_at, place_at = numbers_at(groups, named, SIDE * SIDE)
    half = parts[0].shape[1]
    seq, core = numbers[place_at], numbers[place_at + 1]
    x, z = seq // SIDE, seq % SIDE
    for name in range(groups * named):
        slot = numbers[slots_at + numbers[name]]
        dx = (x - slot // SIDE + SIDE) % SIDE
        dz = (z - slot % SIDE + SIDE) % SIDE
        to = pl.ds(name * LATENTS, LATENTS)
        for side in range(2):
            minor, major = (dx, dz) if side == 0 else (dz, dx)
            start = pl.ds(pl.multiple_of(minor * LATENTS, LATENTS), LATENTS)
            first = jnp.where(core == side, 0, 4)
            for at in range(8):

                @pl.when(first + major == at)
                def _():
                    picked[to, side * half : (side + 1) * half] = parts[at][start, :]

    turned[...] = picked[...].T
    share = turned.shape[0] // (SIDE * SIDE)
    for major in range(SIDE):
        for minor in range(SIDE):
            dx = jnp.where(core == 0, major, minor)
            dz = jnp.where(core == 0, minor, major)
            owner = ((x + dx) % SIDE) * SIDE + (z + dz) % SIDE
            to = (major * SIDE + minor) * share
            picked_t[to : to + share, :] = turned[pl.ds(pl.multiple_of(owner * share, 16), share), :]


def backward(numbers, picked, picked_t, key_weight, value_weight, queries, upstream, query_grad, scratch, groups, named):
    keys, values, key_sum, value_sum, key_part, value_part = scratch
    lengths_at = numbers_at(groups, named, SIDE * SIDE)[1]
    group_keys = named * LATENTS
    group_len = queries.shape[0] // groups
    scale = HEAD_DIM**-0.5
    sharpness = scale * math.log2(math.e)
    keys[...] = jnp.dot(picked[...], key_weight[...], preferred_element_type=F32).astype(BF16)
    values[...] = jnp.dot(picked[...], value_weight[...], preferred_element_type=F32).astype(BF16)
    heads = [slice(head * HEAD_DIM, (head + 1) * HEAD_DIM) for head in range(HEADS)]

    for group in range(groups):
        rows = slice(group * group_keys, (group + 1) * group_keys)
        length = numbers[lengths_at + group]
        blocks = (length + TOKEN_BLOCK - 1) // TOKEN_BLOCK
        key_sum[...] = jnp.zeros_like(key_sum)
        value_sum[...] = jnp.zeros_like(value_sum)

        def block(step, carry):
            at = pl.multiple_of(step * TOKEN_BLOCK, TOKEN_BLOCK)
            tokens = pl.ds(group * group_len + at, TOKEN_BLOCK)
            made = []
            for cols in heads:
                q = queries[tokens, cols]
                dout = upstream[tokens, cols]
                scores = lax.dot_general(keys[rows, cols], q, ONES, preferred_element_type=F32)
                dprob = lax.dot_general(values[rows, cols], dout, ONES, preferred_element_type=F32)
                made.append((cols, q, dout, scores, dprob))
            for cols, q, dout, scores, dprob in made:
                top = jnp.max(scores, axis=0, keepdims=True)
                powers = jnp.exp2((scores - top) * sharpness)
                probs = powers * (1.0 / jnp.sum(powers, axis=0, keepdims=True))
                delta = jnp.sum(probs * dprob, axis=0, keepdims=True)
                dscore = (probs * (dprob - delta)).astype(BF16)
                key_sum[:, cols] += jnp.dot(dscore, q, preferred_element_type=F32)
                value_sum[:, cols] += jnp.dot(probs.astype(BF16), dout, preferred_element_type=F32)
                grad = lax.dot_general(dscore, keys[rows, cols], ZEROS, preferred_element_type=F32)
                query_grad[tokens, cols] = (grad * scale).astype(BF16)
            return carry

        lax.fori_loop(0, blocks, block, 0)

        def blank(step, carry):
            tokens = pl.ds(group * group_len + pl.multiple_of(step * TOKEN_BLOCK, TOKEN_BLOCK), TOKEN_BLOCK)
            query_grad[tokens, :] = jnp.zeros((TOKEN_BLOCK, PAIR), BF16)
            return carry

        lax.fori_loop(blocks, group_len // TOKEN_BLOCK, blank, 0)
        key_part[rows, :] = (key_sum[...] * scale).astype(BF16)
        value_part[rows, :] = value_sum[...].astype(BF16)

    quarter = picked_t.shape[0] // SIDE
    for major in range(SIDE):
        rows = slice(major * quarter, (major + 1) * quarter)
        for part in (key_part, value_part):
            product = jnp.dot(picked_t[rows, :], part[...], preferred_element_type=F32)
            yield major, part is value_part, product.astype(BF16)


def stage_kernel(groups, named, numbers, gate_tanh, key_weight, value_weight, queries, upstream, *refs):
    key_out, value_out, queries_out, dout, numbers_out, raw, copied, arrived = refs
    tokens = upstream.shape[0]
    lengths_at = numbers_at(groups, named, SIDE * SIDE)[1]
    moves = [
        pltpu.make_async_copy(source, target, copied.at[at])
        for at, (source, target) in enumerate(
            ((key_weight, key_out), (value_weight, value_out), (queries, queries_out))
        )
    ]
    chunk = tokens // arrived.shape[0]
    loads = [
        pltpu.make_async_copy(upstream.at[pl.ds(at * chunk, chunk)], raw.at[pl.ds(at * chunk, chunk)], arrived.at[at])
        for at in range(arrived.shape[0])
    ]
    for move in loads + moves:
        move.start()
    for at, load in enumerate(loads):
        load.wait()
        group, first = divmod(at * chunk, tokens // groups)
        rows = slice(at * chunk, (at + 1) * chunk)
        live = lax.broadcasted_iota(jnp.int32, (chunk, upstream.shape[1]), 0) + first < numbers[lengths_at + group]
        dout[rows, :] = jnp.where(live, gate_tanh[...] * raw[rows, :].astype(F32), 0.0).astype(BF16)
    for move in moves:
        move.wait()
    for at in range(numbers.shape[0]):
        numbers_out[at] = numbers[at]


def stage(numbers, gate_tanh, key_weight, value_weight, queries, upstream, groups, named):
    arrays = [pltpu.with_memory_space_constraint(a, pltpu.HBM) for a in (key_weight, value_weight, queries, upstream)]
    return pl.pallas_call(
        functools.partial(stage_kernel, groups, named),
        in_specs=[pl.BlockSpec(memory_space=pltpu.SMEM), pl.BlockSpec(memory_space=pltpu.VMEM)]
        + [pl.BlockSpec(memory_space=pltpu.HBM)] * 4,
        out_specs=[pl.BlockSpec(memory_space=pltpu.VMEM)] * 4 + [pl.BlockSpec(memory_space=pltpu.SMEM)],
        out_shape=[pltpu.VMEM(array.shape, array.dtype) for array in arrays] + [jax.ShapeDtypeStruct(numbers.shape, numbers.dtype)],
        scratch_shapes=[
            pltpu.VMEM(upstream.shape, BF16),
            pltpu.SemaphoreType.DMA((3,)),
            pltpu.SemaphoreType.DMA((8,)),
        ],
        compiler_params=pltpu.CompilerParams(vmem_limit_bytes=24 * 1024 * 1024),
        cost_estimate=pl.CostEstimate(flops=10**7, bytes_accessed=2 * 10**7, transcendentals=0),
    )(numbers, gate_tanh, *arrays)


def first_kernel(groups, named, numbers, *refs):
    parts, staged = refs[:8], [ref.at[:, :PAIR] for ref in refs[8:12]]
    query_grad, messages, (picked, picked_t), turned, scratch = refs[12], refs[13:17], refs[17:19], refs[19], refs[20:]

    @pl.when(pl.program_id(0) == 0)
    def _():
        pick(numbers, parts, picked, turned, picked_t, groups, named)

    share = picked.shape[1] // (SIDE * SIDE)
    for major, second, product in backward(
        numbers, picked, picked_t, *staged, query_grad, scratch, groups, named
    ):
        for minor in range(SIDE):
            to = (2 * minor + second) * share
            messages[major][to : to + share, :] = product[minor * share : (minor + 1) * share]


def second_kernel(groups, named, numbers, *refs):
    picked, picked_t, *staged = refs[:2] + tuple(ref.at[:, PAIR:] for ref in refs[2:6])
    query_grad, messages, scratch = refs[7], refs[8:12], refs[12:]
    share = picked.shape[1] // (SIDE * SIDE)
    for major, second, product in backward(
        numbers, picked, picked_t, *staged, query_grad, scratch, groups, named
    ):
        for minor in range(SIDE):
            to = (2 * minor + second) * share
            messages[major][to : to + share, :] = product[minor * share : (minor + 1) * share]


def attention(numbers, latents, key_weight, value_weight, queries, upstream, query_grad, groups, named):
    first = query_grad is None
    tokens, width = queries.shape
    vision = key_weight.shape[0]
    steps = width // PAIR // 2
    offset = 0 if first else steps
    picked_rows = groups * named * LATENTS
    group_keys = named * LATENTS
    quarter = vision // SIDE
    whole = lambda shape: pl.BlockSpec(shape, lambda step, *_: (0, 0), pipeline_mode=pl.Buffered(1))
    columns = lambda rows: pl.BlockSpec((rows, PAIR), lambda step, *_: (0, step + offset))
    message = lambda rows: pl.BlockSpec((rows, PAIR), lambda step, *_: (0, step))
    shape = jax.ShapeDtypeStruct
    in_specs = [whole(part.shape) for part in latents]
    in_specs += [pl.BlockSpec(memory_space=pltpu.VMEM)] * 4
    staged = [pltpu.with_memory_space_constraint(array, pltpu.VMEM) for array in (key_weight, value_weight, queries, upstream)]
    inputs = [numbers, *latents, *staged]
    out_specs, out_shape = [columns(tokens)], [shape((tokens, width), BF16)]
    scratch = [
        pltpu.VMEM((picked_rows, PAIR), BF16),
        pltpu.VMEM((picked_rows, PAIR), BF16),
        pltpu.VMEM((group_keys, PAIR), F32),
        pltpu.VMEM((group_keys, PAIR), F32),
        pltpu.VMEM((picked_rows, PAIR), BF16),
        pltpu.VMEM((picked_rows, PAIR), BF16),
    ]
    if first:
        out_specs += [message(2 * quarter)] * SIDE + [whole((picked_rows, vision)), whole((vision, picked_rows))]
        out_shape += [shape((2 * quarter, width // 2), BF16)] * SIDE
        out_shape += [shape((picked_rows, vision), BF16), shape((vision, picked_rows), BF16)]
        scratch = [pltpu.VMEM((vision, picked_rows), BF16)] + scratch
        aliases = {}
    else:
        in_specs.append(pl.BlockSpec(memory_space=pl.ANY))
        inputs.append(query_grad)
        out_specs += [message(2 * quarter)] * SIDE
        out_shape += [shape((2 * quarter, width // 2), BF16)] * SIDE
        aliases = {len(inputs) - 1: 0}
    return pl.pallas_call(
        functools.partial(first_kernel if first else second_kernel, groups, named),
        grid_spec=pltpu.PrefetchScalarGridSpec(
            num_scalar_prefetch=1, grid=(steps,), in_specs=in_specs, out_specs=out_specs, scratch_shapes=scratch
        ),
        out_shape=out_shape,
        input_output_aliases=aliases,
        compiler_params=pltpu.CompilerParams(vmem_limit_bytes=28 * 1024 * 1024),
        cost_estimate=pl.CostEstimate(flops=10**10, bytes_accessed=10**7, transcendentals=0),
    )(*inputs)


def add(*arrays):
    return functools.reduce(jnp.add, [array.astype(F32) for array in arrays])


def last_hop(shares, mp):
    return [shares[0]] + [shift(shares[at].astype(BF16), 0, at, mp) for at in (2, 1, 3)]


def finish_kernel(*refs):
    *came, key_grad, value_grad = refs
    rows, width = key_grad.shape[0], key_grad.shape[1] // 2
    for at in range(2):
        total = functools.reduce(jnp.add, [ref[...].astype(F32) for ref in came[at * SIDE : (at + 1) * SIDE]])
        key_grad[:, at * width : (at + 1) * width] = total[:rows]
        value_grad[:, at * width : (at + 1) * width] = total[rows:]


def finish(first, second):
    rows, width = first[0].shape
    return pl.pallas_call(
        finish_kernel,
        out_shape=[jax.ShapeDtypeStruct((rows // 2, 2 * width), F32)] * 2,
        compiler_params=pltpu.CompilerParams(vmem_limit_bytes=8 * 1024 * 1024),
    )(*first, *second)


def local(latents, key_weight, value_weight, queries, upstream, gate, media, frame_slot, lengths, *, mp):
    groups, named = media.shape
    place = jnp.stack([lax.axis_index("seq"), lax.axis_index("mp") % 2]).astype(jnp.int32)
    numbers = jnp.concatenate([media.reshape(-1), frame_slot, lengths, place])
    arrays = (key_weight, value_weight, queries, upstream)
    parts, numbers, rest = gather_latents(latents, numbers, jnp.tanh(gate)[None, :], arrays, groups, named, mp)
    query_grad, *joined, picked, picked_t = attention(numbers, parts, *rest, None, groups, named)
    came = [shift(joined[at], at, 0, mp) for at in (2, 1, 3)]

    query_grad, *messages = attention(numbers, (picked, picked_t), *rest, query_grad, groups, named)
    rows, messages = lax.optimization_barrier((add(joined[0], *came), messages))
    came = [shift(messages[at], at, 0, mp) for at in (2, 1, 3)]
    share = rows.shape[0] // SIDE
    cut = lambda array: [array[at * share : (at + 1) * share] for at in range(SIDE)]
    first = last_hop(cut(rows), mp)
    second = last_hop(cut(add(messages[0], *came)), mp)
    key_grad, value_grad = finish(first, second)
    return query_grad, key_grad, value_grad


def solution(mesh):
    in_specs = (
        P("seq", None),
        P(None, "mp"),
        P(None, "mp"),
        P("seq", "mp"),
        P("seq", "mp"),
        P("mp"),
        P("seq", None),
        P(),
        P("seq"),
    )
    out_specs = (P("seq", "mp"), P("seq", "mp"), P("seq", "mp"))
    body = functools.partial(local, mp=mesh.shape["mp"])
    return jax.shard_map(body, mesh=mesh, in_specs=in_specs, out_specs=out_specs, check_vma=False)
```
